32 devices in a mesh: gx: 4 (over z), gy: 8 (over y, x, core).
Axes of the slice: x: 2, y: 2, z: 4, core: 2. Of those that a mesh axis runs over, the one named last changes fastest.
Arguments:
- speed_factor: float32 [64, 128, 256], P('gx', 'gy'), may hold values from 0.05 to 0.17
- wave_before: float32 [64, 128, 256], P('gx', 'gy'), may hold values from -6 to 6
- wave_now: float32 [64, 128, 256], P('gx', 'gy'), may hold values from -6 to 6
- source_accel: float32 [2, 64, 128, 256], P(None, 'gx', 'gy'), may hold values from -4 to 4
- prior_image: float32 [64, 128, 256], P('gx', 'gy'), may hold values from -40 to 40
- conv_first: bfloat16 [27, 1, 8], replicated, may hold values from -1.25 to 1.25
- bias_first: float32 [8], replicated, may hold values from -3 to 3
- conv_middle: bfloat16 [27, 8, 8], replicated, may hold values from -0.4375 to 0.4375
- bias_middle: float32 [8], replicated, may hold values from -3 to 3
- conv_last: bfloat16 [27, 8, 1], replicated, may hold values from -0.4375 to 0.4375
Outputs:
- wave_next: float32 [64, 128, 256], P('gx', 'gy')
- wave_after: float32 [64, 128, 256], P('gx', 'gy')
- gradient: float32 [64, 128, 256], P('gx', 'gy')
- model_step: float32 [64, 128, 256], P('gx', 'gy')
The draws below stay inside these ranges and needn't reach their ends.
All inputs are finite; a program needn't handle non-finite values.
Results may differ from the reference program's by a relative error of at most 0.0059.
Values may be sent and summed in bfloat16 or wider, within the bound.
A program may use at most 192 MiB of HBM per device.

```python
import jax
import jax.numpy as jnp
from jax import lax

NZ = 256
CH = 8
NX = 64
NY = 128


def draw_prior_image(key, part):
    along_x = 1.0 + 2.0 * jnp.arange(NX, dtype=jnp.float32) / NX
    along_y = 1.0 + 2.0 * jnp.arange(NY, dtype=jnp.float32) / NY
    scale = along_x[:, None, None] * along_y[None, :, None]
    return scale * jnp.clip(jax.random.normal(key, (NX, NY, NZ), jnp.float32), -4.0, 4.0)


def block_scale(own_key, extent, pieces, smallest, top_value):
    gain = 1.0
    for position, parts in pieces:
        steps = jax.random.uniform(jax.random.fold_in(jax.random.fold_in(own_key, 6), position), (parts,), jnp.float32, smallest / len(pieces), top_value / len(pieces))
        gain = gain * jnp.repeat(jnp.exp(steps), extent[position] // parts).reshape((-1,) + (1,) * (len(extent) - 1 - position))
    return gain


def gaussian(stream_key, shape, width, limit, shards=(), held_as=jnp.bfloat16):
    loudness = block_scale(stream_key, shape, shards, -0.22, 0.18) if shards else 1.0
    array = jax.random.normal(stream_key, shape, jnp.float32) * width * loudness
    return jnp.minimum(jnp.maximum(array, -limit), limit).astype(held_as)


def setup_inputs(seed: int = 0) -> dict:
    keys = jax.random.split(jax.random.key(seed), 11)
    speed_factor = jnp.clip(0.05 + 0.12000000104308128 * jax.random.uniform(keys[0], (NX, NY, NZ), jnp.float32) ** block_scale(keys[0], (NX, NY, NZ), ((0, 4), (1, 8)), -0.2, 0.2), 0.05, 0.17)
    wave_before = gaussian(keys[1], (NX, NY, NZ), 1.0, 6.0, ((0, 4), (1, 8)), jnp.float32)
    wave_now = gaussian(keys[2], (NX, NY, NZ), 1.0, 6.0, ((0, 4), (1, 8)), jnp.float32)
    source_accel = gaussian(keys[3], (2, NX, NY, NZ), 0.5, 4.0, ((1, 4), (2, 8)), jnp.float32)
    prior_image = draw_prior_image(jax.random.fold_in(keys[10], 71), 0)
    conv_first = gaussian(keys[5], (27, 1, CH), 27 ** -0.5, 1.25)
    bias_first = gaussian(keys[6], (CH,), 0.5, 3.0, (), jnp.float32)
    conv_middle = gaussian(keys[7], (27, CH, CH), (27 * CH) ** -0.5, 0.4375)
    bias_middle = gaussian(keys[8], (CH,), 0.5, 3.0, (), jnp.float32)
    conv_last = gaussian(keys[9], (27, CH, 1), (27 * CH) ** -0.5, 0.4375)
    return dict(speed_factor=speed_factor, wave_before=wave_before, wave_now=wave_now, source_accel=source_accel, prior_image=prior_image, conv_first=conv_first, bias_first=bias_first, conv_middle=conv_middle, bias_middle=bias_middle, conv_last=conv_last)


COEFS = (-205.0 / 72.0, 8.0 / 5.0, -1.0 / 5.0, 8.0 / 315.0, -1.0 / 560.0)


def laplace(field):
    padded = jnp.pad(field, 4)
    size_x, size_y, size_z = field.shape
    total = 3.0 * COEFS[0] * field
    for reach in range(1, 5):
        cycle = padded[4 + reach:4 + reach + size_x, 4:4 + size_y, 4:4 + size_z]
        cycle = cycle + padded[4 - reach:4 - reach + size_x, 4:4 + size_y, 4:4 + size_z]
        cycle = cycle + padded[4:4 + size_x, 4 + reach:4 + reach + size_y, 4:4 + size_z]
        cycle = cycle + padded[4:4 + size_x, 4 - reach:4 - reach + size_y, 4:4 + size_z]
        cycle = cycle + padded[4:4 + size_x, 4:4 + size_y, 4 + reach:4 + reach + size_z]
        cycle = cycle + padded[4:4 + size_x, 4:4 + size_y, 4 - reach:4 - reach + size_z]
        total = total + COEFS[reach] * cycle
    return total


def conv_layer(inputs, weight):
    kernel = weight.astype(jnp.float32).reshape(3, 3, 3, weight.shape[1], weight.shape[2])
    kernel = kernel.transpose(4, 3, 0, 1, 2)
    result = lax.conv_general_dilated(inputs.astype(jnp.float32)[None], kernel, (1, 1, 1), "SAME",
                                      dimension_numbers=("NCDHW", "OIDHW", "NCDHW"),
                                      precision=lax.Precision.HIGHEST)
    return result[0]


def reference(speed_factor, wave_before, wave_now, source_accel, prior_image, conv_first, bias_first, conv_middle, bias_middle, conv_last):
    wave_next = 2.0 * wave_now - wave_before + speed_factor * laplace(wave_now)
    wave_after = 2.0 * wave_next - wave_now + speed_factor * laplace(wave_next)
    gradient = prior_image + source_accel[0] * wave_next + source_accel[1] * wave_after
    layer_in = gradient.astype(jnp.bfloat16)[None]
    hidden_one = jnp.maximum(conv_layer(layer_in, conv_first) + bias_first[:, None, None, None], 0.0).astype(jnp.bfloat16)
    hidden_two = jnp.maximum(conv_layer(hidden_one, conv_middle) + bias_middle[:, None, None, None], 0.0).astype(jnp.bfloat16)
    direction = conv_layer(hidden_two, conv_last)[0] + gradient
    sum_gg = jnp.sum(gradient * gradient)
    sum_gd = jnp.sum(gradient * direction)
    sum_dd = jnp.sum(direction * direction)
    damping = 8.0 * float(NX * NY * NZ)
    model_step = (sum_gd / (sum_gg + sum_dd + damping)) * direction
    return wave_next, wave_after, gradient, model_step
```

```python
import functools

import jax
import jax.numpy as jnp
from jax import lax
from jax.experimental import pallas as pl
from jax.experimental.pallas import tpu as pltpu
from jax.sharding import PartitionSpec as P

COEFS = (-205.0 / 72.0, 8.0 / 5.0, -1.0 / 5.0, 8.0 / 315.0, -1.0 / 560.0)
MESH = pl.DeviceIdType.MESH
F32 = jnp.float32
BF16 = jnp.bfloat16


def shift_z(v, k):
    depth = v.shape[-1]
    lane = lax.broadcasted_iota(jnp.int32, v.shape, v.ndim - 1)
    rolled = pltpu.roll(v, (-k) % depth, v.ndim - 1)
    return jnp.where((lane + k >= 0) & (lane + k < depth), rolled, 0.0)


def laplace_plane(ext, x, ny):
    center = ext[x + 4, 8 : 8 + ny, :]
    total = 3.0 * COEFS[0] * center
    for k in range(1, 5):
        cycle = ext[x + 4 + k, 8 : 8 + ny, :] + ext[x + 4 - k, 8 : 8 + ny, :]
        cycle = cycle + ext[x + 4, 8 + k : 8 + k + ny, :]
        cycle = cycle + ext[x + 4, 8 - k : 8 - k + ny, :]
        cycle = cycle + shift_z(center, k) + shift_z(center, -k)
        total = total + COEFS[k] * cycle
    return center, total


def kernel(
    n_gx,
    n_gy,
    speed,
    before,
    now,
    src,
    prior,
    s1,
    s2,
    s3,
    b1,
    b2,
    out_next,
    out_after,
    out_grad,
    out_step,
    ext_a,
    ext_b,
    pack_a,
    pack_b,
    recv_a,
    recv_b,
    grad,
    pack_g,
    recv_g,
    h1,
    h2,
    w1,
    w2,
    w3,
    part,
    red_y,
    red_x,
    send_sem,
    recv_sem,
    ry_send,
    ry_recv,
    rx_send,
    rx_recv,
):
    nx, ny, depth = now.shape
    gx, gy = lax.axis_index("gx"), lax.axis_index("gy")
    barrier = pltpu.get_barrier_semaphore()

    def there(dx, dy):
        ok = None
        for pos, d, n in ((gx, dx, n_gx), (gy, dy, n_gy)):
            if d:
                one = (pos + d >= 0) & (pos + d < n)
                ok = one if ok is None else ok & one
        return ok

    for i in range(1, n_gy):
        pl.semaphore_signal(
            barrier, inc=1, device_id=(gx, lax.rem(gy + i, n_gy)), device_id_type=MESH
        )
    for i in range(1, n_gx):
        pl.semaphore_signal(
            barrier, inc=1, device_id=(lax.rem(gx + i, n_gx), gy), device_id_type=MESH
        )
    diagonals = ((-1, -1), (-1, 1), (1, -1), (1, 1))
    for dx, dy in diagonals:

        @pl.when(there(dx, dy))
        def _(dx=dx, dy=dy):
            pl.semaphore_signal(barrier, inc=1, device_id=(gx + dx, gy + dy), device_id_type=MESH)

    class Copy:
        def __init__(self, ident, source, target, dx, dy):
            self.make = lambda: pltpu.make_async_remote_copy(
                src_ref=source,
                dst_ref=target,
                send_sem=send_sem.at[ident],
                recv_sem=recv_sem.at[ident],
                device_id=(gx + dx, gy + dy),
                device_id_type=MESH,
            )
            self.to = there(dx, dy)
            self.origin = there(-dx, -dy)
            self.target = target

        def start(self):
            @pl.when(self.to)
            def _():
                self.make().start()

        def clear(self):
            @pl.when(jnp.logical_not(self.origin))
            def _():
                self.target[...] = jnp.zeros(self.target.shape, self.target.dtype)

        def arrive(self):
            @pl.when(self.origin)
            def _():
                self.make().wait_recv()

        def sent(self):
            @pl.when(self.to)
            def _():
                self.make().wait_send()

    own = pl.ds(8, ny)

    def wave_copies(base, ext, pack, recv):
        return (
            Copy(base, ext.at[pl.ds(nx, 4), own, :], ext.at[pl.ds(0, 4), own, :], 1, 0),
            Copy(base + 1, ext.at[pl.ds(4, 4), own, :], ext.at[pl.ds(nx + 4, 4), own, :], -1, 0),
            Copy(base + 2, pack.at[1], recv.at[0], 0, 1),
            Copy(base + 3, pack.at[0], recv.at[1], 0, -1),
        )

    copies_a = wave_copies(0, ext_a, pack_a, recv_a)
    copies_b = wave_copies(4, ext_b, pack_b, recv_b)
    row16 = pl.ds(0, ny)
    groups = nx // 4
    mid = pl.ds(1, groups)
    copies_g = (
        Copy(8, grad.at[pl.ds(nx, 4), row16, :], grad.at[pl.ds(0, 4), row16, :], 1, 0),
        Copy(9, grad.at[pl.ds(4, 4), row16, :], grad.at[pl.ds(nx + 4, 4), row16, :], -1, 0),
        Copy(10, pack_g.at[1], recv_g.at[0, mid], 0, 1),
        Copy(11, pack_g.at[0], recv_g.at[1, mid], 0, -1),
        Copy(12, pack_g.at[1, groups - 1], recv_g.at[0, 0], 1, 1),
        Copy(13, pack_g.at[1, 0], recv_g.at[0, groups + 1], -1, 1),
        Copy(14, pack_g.at[0, groups - 1], recv_g.at[1, 0], 1, -1),
        Copy(15, pack_g.at[0, 0], recv_g.at[1, groups + 1], -1, -1),
    )

    def pack_wave(ext, pack):
        half = nx // 2
        for i in range(half):
            for side, at in ((0, 8), (1, 8 + ny - 4)):
                pack[side, i] = jnp.concatenate(
                    [ext[4 + i, at : at + 4, :], ext[4 + half + i, at : at + 4, :]], axis=0
                )

    def unpack_wave(ext, recv):
        half = nx // 2
        for i in range(half):
            for side, at in ((0, 4), (1, 8 + ny)):
                tile = recv[side, i]
                ext[4 + i, at : at + 4, :] = tile[0:4]
                ext[4 + half + i, at : at + 4, :] = tile[4:8]

    ext_a[pl.ds(4, nx), own, :] = now[...]
    pack_wave(ext_a, pack_a)
    for group in (copies_a, copies_b, copies_g):
        for c in group:
            c.clear()

    wanted = (n_gy - 1) + (n_gx - 1)
    for dx, dy in diagonals:
        wanted = wanted + there(dx, dy).astype(jnp.int32)
    pl.semaphore_wait(barrier, wanted)
    for c in copies_a:
        c.start()

    def band(out, slabs, e, rows, per_row, first_out, width, place):
        shape = (rows * per_row, 3 * width)
        col = lax.broadcasted_iota(jnp.int32, shape, 1)
        row = lax.broadcasted_iota(jnp.int32, shape, 0)
        slot = col - jnp.where(col >= width, width, 0) - jnp.where(col >= 2 * width, width, 0)
        y_out = (row >> 3 if per_row == 8 else row) + first_out
        gap = place(slot) - y_out
        total = jnp.zeros(shape, F32)
        for b in range(3):
            slab = slabs[3 * b + e]
            if per_row == 8:
                full = jnp.concatenate([slab] * rows, axis=0)
            else:
                full = jnp.broadcast_to(slab, shape)
            total = jnp.where(gap == b - 1, full, total)
        out[e * shape[0] : (e + 1) * shape[0], :] = total.astype(BF16)

    def grad_slot(slot):
        return jnp.where(
            slot < ny, slot, jnp.where(slot < ny + 4, slot - ny - 4, jnp.where(slot < ny + 8, slot - 4, 999))
        )

    r1, r2 = ny + 4, ny + 2
    for e in range(3):
        band(w1, s1, e, r1, 8, -2, 2 * ny, grad_slot)
        band(w2, s2, e, r2, 8, -1, r1 * 8, lambda s: (s >> 3) - 2)
        band(w3, s3, e, ny, 1, 0, r2 * 8, lambda s: (s >> 3) - 1)

    for c in copies_a:
        c.arrive()
    unpack_wave(ext_a, recv_a)

    def step_one(x, carry):
        center, lap = laplace_plane(ext_a, x, ny)
        value = 2.0 * center - before[x] + speed[x] * lap
        out_next[x] = value
        ext_b[x + 4, 8 : 8 + ny, :] = value
        return carry

    lax.fori_loop(0, nx, step_one, 0)
    pack_wave(ext_b, pack_b)
    for c in copies_b:
        c.start()
    for c in copies_b:
        c.arrive()
    unpack_wave(ext_b, recv_b)

    def step_two(x, carry):
        center, lap = laplace_plane(ext_b, x, ny)
        value = 2.0 * center - now[x] + speed[x] * lap
        out_after[x] = value
        gradient = prior[x] + src[0, x] * center + src[1, x] * value
        out_grad[x] = gradient
        grad[x + 4, 0:ny, :] = gradient.astype(BF16)
        return carry

    lax.fori_loop(0, nx, step_two, 0)
    for t in range(groups):
        for side, at in ((0, 0), (1, ny - 4)):
            pack_g[side, t] = jnp.concatenate(
                [out_grad[4 * t + j, at : at + 4, :] for j in range(4)], axis=0
            ).astype(BF16)
    for c in copies_g:
        c.start()
    for c in copies_g:
        c.arrive()
    for t in range(groups + 2):
        low = recv_g[0, t].astype(F32)
        high = recv_g[1, t].astype(F32)
        for j in range(4):
            grad[4 * t + j, ny : 2 * ny, :] = jnp.concatenate(
                [low[4 * j : 4 * j + 4], high[4 * j : 4 * j + 4], jnp.zeros((ny - 8, depth), F32)],
                axis=0,
            ).astype(BF16)

    x_min = jnp.where(gx == 0, 0, -8)
    x_max = jnp.where(gx == n_gx - 1, nx, nx + 8)
    y_min = jnp.where(gy == 0, 0, -8)
    y_max = jnp.where(gy == n_gy - 1, ny, ny + 8)

    def conv_plane(weight, rhs, rows):
        res = jnp.dot(weight[...], rhs, preferred_element_type=F32)
        return (
            res[rows : 2 * rows] + shift_z(res[:rows], -1) + shift_z(res[2 * rows :], 1)
        )

    def hidden(value, bias, rows, first, x):
        y = (lax.broadcasted_iota(jnp.int32, value.shape, 0) >> 3) + first
        inside = (y >= y_min) & (y < y_max) & (x >= x_min) & (x < x_max)
        full = jnp.concatenate([jnp.broadcast_to(bias[...], (8, depth))] * rows, axis=0)
        return jnp.where(inside, jnp.maximum(value + full, 0.0), 0.0).astype(BF16)

    m1, m2 = 8 * r1, 8 * r2

    def layer_one(p, carry):
        rhs = grad[pl.ds(p + 1, 3)].reshape(6 * ny, depth)
        h1[p] = hidden(conv_plane(w1, rhs, m1), b1, r1, -2, p - 2)
        return carry

    lax.fori_loop(0, nx + 4, layer_one, 0)

    def layer_two(p, carry):
        rhs = h1[pl.ds(p, 3)].reshape(3 * m1, depth)
        h2[p] = hidden(conv_plane(w2, rhs, m2), b2, r2, -1, p - 1)
        return carry

    lax.fori_loop(0, nx + 2, layer_two, 0)

    zero = jnp.zeros((ny, depth), F32)

    def layer_three(p, carry):
        gg, gd, dd = carry
        rhs = h2[pl.ds(p, 3)].reshape(3 * m2, depth)
        g = out_grad[p]
        d = conv_plane(w3, rhs, ny) + g
        out_step[p] = d
        return gg + g * g, gd + g * d, dd + d * d

    sums = lax.fori_loop(0, nx, layer_three, (zero, zero, zero))
    row = lax.broadcasted_iota(jnp.int32, (8, depth), 0)
    tile = jnp.zeros((8, depth), F32)
    for i, s in enumerate(sums):
        tile = jnp.where(row == i, jnp.sum(s, axis=0, keepdims=True), tile)
    folded = tile[:, 0:128]
    for i in range(1, depth // 128):
        folded = folded + tile[:, 128 * i : 128 * i + 128]

    def reduce_over(value, slot, slots, me, n, sends, recvs, peer_id):
        part[slot] = value
        slots[me] = value
        todo = []
        for i in range(1, n):
            c = pltpu.make_async_remote_copy(
                src_ref=part.at[slot],
                dst_ref=slots.at[me],
                send_sem=sends.at[i],
                recv_sem=recvs.at[i],
                device_id=peer_id(lax.rem(me + i, n)),
                device_id_type=MESH,
            )
            c.start()
            todo.append(c)
        for i, c in enumerate(todo):
            back = pltpu.make_async_remote_copy(
                src_ref=part.at[slot],
                dst_ref=slots.at[lax.rem(me + n - (i + 1), n)],
                send_sem=sends.at[i + 1],
                recv_sem=recvs.at[i + 1],
                device_id=peer_id(lax.rem(me + i + 1, n)),
                device_id_type=MESH,
            )
            back.wait_recv()
        total = slots[0]
        for i in range(1, n):
            total = total + slots[i]
        return total, todo

    over_y, todo_y = reduce_over(folded, 0, red_y, gy, n_gy, ry_send, ry_recv, lambda j: (gx, j))
    total, todo_x = reduce_over(over_y, 1, red_x, gx, n_gx, rx_send, rx_recv, lambda j: (j, gy))
    sums = jnp.sum(total, axis=1, keepdims=True)
    damping = 8.0 * float(nx * n_gx * ny * n_gy * depth)
    scale = sums[1:2] / (sums[0:1] + sums[2:3] + damping)

    def finish(p, carry):
        out_step[p] = scale * out_step[p]
        return carry

    lax.fori_loop(0, nx, finish, 0)
    for group in (copies_a, copies_b, copies_g):
        for c in group:
            c.sent()
    for c in todo_y + todo_x:
        c.wait_send()


def slabs(weight, slots):
    _, c, d = weight.shape
    w = weight.astype(F32).reshape(3, 9, c, d).transpose(1, 3, 0, 2)
    w = jnp.broadcast_to(w[:, :, :, None, :], (9, d, 3, slots, c))
    return w.reshape(9, d, 3 * slots * c)


def shards(n_gx, n_gy, speed, before, now, src, prior, w_first, b_first, w_mid, b_mid, w_last):
    nx, ny, depth = now.shape
    out = jax.ShapeDtypeStruct(now.shape, F32)
    vmem = pl.BlockSpec(memory_space=pltpu.VMEM)
    half, groups = nx // 2, nx // 4
    r1, r2 = ny + 4, ny + 2
    ch = b_first.shape[0]
    return pl.pallas_call(
        functools.partial(kernel, n_gx, n_gy),
        out_shape=(out,) * 4,
        in_specs=[vmem] * 10,
        out_specs=(vmem,) * 4,
        scratch_shapes=[
            pltpu.VMEM((nx + 8, ny + 16, depth), F32),
            pltpu.VMEM((nx + 8, ny + 16, depth), F32),
            pltpu.VMEM((2, half, 8, depth), F32),
            pltpu.VMEM((2, half, 8, depth), F32),
            pltpu.VMEM((2, half, 8, depth), F32),
            pltpu.VMEM((2, half, 8, depth), F32),
            pltpu.VMEM((nx + 8, 2 * ny, depth), BF16),
            pltpu.VMEM((2, groups, 16, depth), BF16),
            pltpu.VMEM((2, groups + 2, 16, depth), BF16),
            pltpu.VMEM((nx + 4, r1 * ch, depth), BF16),
            pltpu.VMEM((nx + 2, r2 * ch, depth), BF16),
            pltpu.VMEM((3 * r1 * ch, 6 * ny), BF16),
            pltpu.VMEM((3 * r2 * ch, 3 * r1 * ch), BF16),
            pltpu.VMEM((3 * ny, 3 * r2 * ch), BF16),
            pltpu.VMEM((2, 8, 128), F32),
            pltpu.VMEM((n_gy, 8, 128), F32),
            pltpu.VMEM((n_gx, 8, 128), F32),
            pltpu.SemaphoreType.DMA((16,)),
            pltpu.SemaphoreType.DMA((16,)),
            pltpu.SemaphoreType.DMA((n_gy,)),
            pltpu.SemaphoreType.DMA((n_gy,)),
            pltpu.SemaphoreType.DMA((n_gx,)),
            pltpu.SemaphoreType.DMA((n_gx,)),
        ],
        compiler_params=pltpu.CompilerParams(
            collective_id=0, has_side_effects=True, vmem_limit_bytes=40 * 1024 * 1024
        ),
    )(
        speed,
        before,
        now,
        src,
        prior,
        slabs(w_first, 2 * ny),
        slabs(w_mid, r1),
        slabs(w_last, r2),
        b_first.reshape(ch, 1),
        b_mid.reshape(ch, 1),
    )


def solution(mesh):
    brick = P("gx", "gy", None)
    return jax.shard_map(
        functools.partial(shards, mesh.shape["gx"], mesh.shape["gy"]),
        mesh=mesh,
        in_specs=(brick, brick, brick, P(None, "gx", "gy", None), brick, P(), P(), P(), P(), P()),
        out_specs=(brick,) * 4,
        check_vma=False,
    )
```

```python
import functools

import jax
import jax.numpy as jnp
from jax import lax
from jax.experimental import pallas as pl
from jax.experimental.pallas import tpu as pltpu
from jax.sharding import PartitionSpec as P

COEFS = (-205.0 / 72.0, 8.0 / 5.0, -1.0 / 5.0, 8.0 / 315.0, -1.0 / 560.0)
MESH = pl.DeviceIdType.MESH
F32 = jnp.float32
BF16 = jnp.bfloat16
UNROLL = True
WAVE_UNROLL = 4


def shift_z(v, k):
    depth = v.shape[-1]
    lane = lax.broadcasted_iota(jnp.int32, v.shape, v.ndim - 1)
    rolled = pltpu.roll(v, (-k) % depth, v.ndim - 1)
    return jnp.where((lane + k >= 0) & (lane + k < depth), rolled, 0.0)


def laplace_plane(ext, x, ny):
    center = ext[x + 4, 8 : 8 + ny, :]
    total = 3.0 * COEFS[0] * center
    for k in range(1, 5):
        cycle = ext[x + 4 + k, 8 : 8 + ny, :] + ext[x + 4 - k, 8 : 8 + ny, :]
        cycle = cycle + ext[x + 4, 8 + k : 8 + k + ny, :]
        cycle = cycle + ext[x + 4, 8 - k : 8 - k + ny, :]
        cycle = cycle + shift_z(center, k) + shift_z(center, -k)
        total = total + COEFS[k] * cycle
    return center, total


def kernel(
    n_gx,
    n_gy,
    speed,
    before,
    now,
    src,
    prior,
    s1,
    s2,
    s3,
    b1,
    b2,
    out_next,
    out_after,
    out_grad,
    out_step,
    ext_a,
    ext_b,
    pack_a,
    pack_b,
    recv_a,
    recv_b,
    grad,
    pack_g,
    recv_g,
    h1,
    h2,
    w1,
    w2,
    w3,
    part,
    red_y,
    red_x,
    send_sem,
    recv_sem,
    ry_send,
    ry_recv,
    rx_send,
    rx_recv,
):
    nx, ny, depth = now.shape
    gx, gy = lax.axis_index("gx"), lax.axis_index("gy")
    barrier = pltpu.get_barrier_semaphore()

    def there(dx, dy):
        ok = None
        for pos, d, n in ((gx, dx, n_gx), (gy, dy, n_gy)):
            if d:
                one = (pos + d >= 0) & (pos + d < n)
                ok = one if ok is None else ok & one
        return ok

    for i in range(1, n_gy):
        pl.semaphore_signal(
            barrier, inc=1, device_id=(gx, lax.rem(gy + i, n_gy)), device_id_type=MESH
        )
    for i in range(1, n_gx):
        pl.semaphore_signal(
            barrier, inc=1, device_id=(lax.rem(gx + i, n_gx), gy), device_id_type=MESH
        )
    diagonals = ((-1, -1), (-1, 1), (1, -1), (1, 1))
    for dx, dy in diagonals:

        @pl.when(there(dx, dy))
        def _(dx=dx, dy=dy):
            pl.semaphore_signal(barrier, inc=1, device_id=(gx + dx, gy + dy), device_id_type=MESH)

    class Copy:
        def __init__(self, ident, source, target, dx, dy):
            self.make = lambda: pltpu.make_async_remote_copy(
                src_ref=source,
                dst_ref=target,
                send_sem=send_sem.at[ident],
                recv_sem=recv_sem.at[ident],
                device_id=(gx + dx, gy + dy),
                device_id_type=MESH,
            )
            self.to = there(dx, dy)
            self.origin = there(-dx, -dy)
            self.target = target

        def start(self):
            @pl.when(self.to)
            def _():
                self.make().start()

        def clear(self):
            @pl.when(jnp.logical_not(self.origin))
            def _():
                self.target[...] = jnp.zeros(self.target.shape, self.target.dtype)

        def arrive(self):
            @pl.when(self.origin)
            def _():
                self.make().wait_recv()

        def sent(self):
            @pl.when(self.to)
            def _():
                self.make().wait_send()

    own = pl.ds(8, ny)

    def wave_copies(base, ext, pack, recv):
        return (
            Copy(base, ext.at[pl.ds(nx, 4), own, :], ext.at[pl.ds(0, 4), own, :], 1, 0),
            Copy(base + 1, ext.at[pl.ds(4, 4), own, :], ext.at[pl.ds(nx + 4, 4), own, :], -1, 0),
            Copy(base + 2, pack.at[1], recv.at[0], 0, 1),
            Copy(base + 3, pack.at[0], recv.at[1], 0, -1),
        )

    copies_a = wave_copies(0, ext_a, pack_a, recv_a)
    copies_b = wave_copies(4, ext_b, pack_b, recv_b)
    row16 = pl.ds(0, ny)
    groups = nx // 4
    mid = pl.ds(1, groups)
    copies_g = (
        Copy(8, grad.at[pl.ds(nx, 4), row16, :], grad.at[pl.ds(0, 4), row16, :], 1, 0),
        Copy(9, grad.at[pl.ds(4, 4), row16, :], grad.at[pl.ds(nx + 4, 4), row16, :], -1, 0),
        Copy(10, pack_g.at[1], recv_g.at[0, mid], 0, 1),
        Copy(11, pack_g.at[0], recv_g.at[1, mid], 0, -1),
        Copy(12, pack_g.at[1, groups - 1], recv_g.at[0, 0], 1, 1),
        Copy(13, pack_g.at[1, 0], recv_g.at[0, groups + 1], -1, 1),
        Copy(14, pack_g.at[0, groups - 1], recv_g.at[1, 0], 1, -1),
        Copy(15, pack_g.at[0, 0], recv_g.at[1, groups + 1], -1, -1),
    )

    def pack_wave(ext, pack):
        half = nx // 2
        for i in range(half):
            for side, at in ((0, 8), (1, 8 + ny - 4)):
                pack[side, i] = jnp.concatenate(
                    [ext[4 + i, at : at + 4, :], ext[4 + half + i, at : at + 4, :]], axis=0
                )

    def unpack_wave(ext, recv):
        half = nx // 2
        for i in range(half):
            for side, at in ((0, 4), (1, 8 + ny)):
                tile = recv[side, i]
                ext[4 + i, at : at + 4, :] = tile[0:4]
                ext[4 + half + i, at : at + 4, :] = tile[4:8]

    ext_a[pl.ds(4, nx), own, :] = now[...]
    pack_wave(ext_a, pack_a)
    for group in (copies_a, copies_b, copies_g):
        for c in group:
            c.clear()

    wanted = (n_gy - 1) + (n_gx - 1)
    for dx, dy in diagonals:
        wanted = wanted + there(dx, dy).astype(jnp.int32)
    pl.semaphore_wait(barrier, wanted)
    for c in copies_a:
        c.start()

    def band(out, slabs, e, rows, per_row, first_out, width, place):
        shape = (rows * per_row, 3 * width)
        col = lax.broadcasted_iota(jnp.int32, shape, 1)
        row = lax.broadcasted_iota(jnp.int32, shape, 0)
        slot = col - jnp.where(col >= width, width, 0) - jnp.where(col >= 2 * width, width, 0)
        y_out = (row >> 3 if per_row == 8 else row) + first_out
        gap = place(slot) - y_out
        total = jnp.zeros(shape, F32)
        for b in range(3):
            slab = slabs[3 * b + e]
            if per_row == 8:
                full = jnp.concatenate([slab] * rows, axis=0)
            else:
                full = jnp.broadcast_to(slab, shape)
            total = jnp.where(gap == b - 1, full, total)
        out[e * shape[0] : (e + 1) * shape[0], :] = total.astype(BF16)

    def grad_slot(slot):
        return jnp.where(
            slot < ny, slot, jnp.where(slot < ny + 4, slot - ny - 4, jnp.where(slot < ny + 8, slot - 4, 999))
        )

    r1, r2 = ny + 4, ny + 2
    m1, m2 = 8 * r1, 8 * r2
    wide = 3 * m1
    col = lax.broadcasted_iota(jnp.int32, (24, wide), 1)
    row = lax.broadcasted_iota(jnp.int32, (24, wide), 0)
    col_a = jnp.where(col >= m1, 1, 0) + jnp.where(col >= 2 * m1, 1, 0)
    pick = jnp.where(row == 8 * col_a + (col & 7), 1.0, 0.0).astype(BF16)
    s2_wide = jnp.dot(s2[...], pick, preferred_element_type=F32)
    s2_slabs = [s2_wide[8 * k : 8 * k + 8] for k in range(9)]
    for e in range(3):
        band(w1, s1, e, r1, 8, -2, 2 * ny, grad_slot)
        band(w2, s2_slabs, e, r2, 8, -1, r1 * 8, lambda s: (s >> 3) - 2)
        band(w3, s3, e, ny, 1, 0, r2 * 8, lambda s: (s >> 3) - 1)

    for c in copies_a:
        c.arrive()
    unpack_wave(ext_a, recv_a)

    def step_one(x, carry):
        center, lap = laplace_plane(ext_a, x, ny)
        value = 2.0 * center - before[x] + speed[x] * lap
        out_next[x] = value
        ext_b[x + 4, 8 : 8 + ny, :] = value
        return carry

    lax.fori_loop(0, nx, step_one, 0, unroll=WAVE_UNROLL)
    pack_wave(ext_b, pack_b)
    for c in copies_b:
        c.start()
    for c in copies_b:
        c.arrive()
    unpack_wave(ext_b, recv_b)

    def step_two(x, carry):
        center, lap = laplace_plane(ext_b, x, ny)
        value = 2.0 * center - now[x] + speed[x] * lap
        out_after[x] = value
        gradient = prior[x] + src[0, x] * center + src[1, x] * value
        out_grad[x] = gradient
        grad[x + 4, 0:ny, :] = gradient.astype(BF16)
        return carry

    lax.fori_loop(0, nx, step_two, 0, unroll=WAVE_UNROLL)
    for t in range(groups):
        for side, at in ((0, 0), (1, ny - 4)):
            pack_g[side, t] = jnp.concatenate(
                [out_grad[4 * t + j, at : at + 4, :] for j in range(4)], axis=0
            ).astype(BF16)
    for c in copies_g:
        c.start()
    for c in copies_g:
        c.arrive()
    for t in range(groups + 2):
        low = recv_g[0, t].astype(F32)
        high = recv_g[1, t].astype(F32)
        for j in range(4):
            grad[4 * t + j, ny : 2 * ny, :] = jnp.concatenate(
                [low[4 * j : 4 * j + 4], high[4 * j : 4 * j + 4], jnp.zeros((ny - 8, depth), F32)],
                axis=0,
            ).astype(BF16)

    x_min = jnp.where(gx == 0, 0, -8)
    x_max = jnp.where(gx == n_gx - 1, nx, nx + 8)
    y_min = jnp.where(gy == 0, 0, -8)
    y_max = jnp.where(gy == n_gy - 1, ny, ny + 8)

    def conv_plane(weight, rhs, rows):
        res = jnp.dot(weight[...], rhs, preferred_element_type=F32)
        return (
            res[rows : 2 * rows] + shift_z(res[:rows], -1) + shift_z(res[2 * rows :], 1)
        )

    def hidden(value, bias, rows, first, x):
        y = (lax.broadcasted_iota(jnp.int32, value.shape, 0) >> 3) + first
        inside = (y >= y_min) & (y < y_max) & (x >= x_min) & (x < x_max)
        full = jnp.concatenate([jnp.broadcast_to(bias[...], (8, depth))] * rows, axis=0)
        return jnp.where(inside, jnp.maximum(value + full, 0.0), 0.0).astype(BF16)

    def layer_one(p, carry):
        rhs = grad[pl.ds(p + 1, 3)].reshape(6 * ny, depth)
        h1[p] = hidden(conv_plane(w1, rhs, m1), b1, r1, -2, p - 2)
        return carry

    lax.fori_loop(0, nx + 4, layer_one, 0, unroll=UNROLL)

    def layer_two(p, carry):
        rhs = h1[pl.ds(p, 3)].reshape(3 * m1, depth)
        h2[p] = hidden(conv_plane(w2, rhs, m2), b2, r2, -1, p - 1)
        return carry

    lax.fori_loop(0, nx + 2, layer_two, 0, unroll=UNROLL)

    zero = jnp.zeros((ny, depth), F32)

    def layer_three(p, carry):
        gg, gd, dd = carry
        rhs = h2[pl.ds(p, 3)].reshape(3 * m2, depth)
        g = out_grad[p]
        d = conv_plane(w3, rhs, ny) + g
        out_step[p] = d
        return gg + g * g, gd + g * d, dd + d * d

    sums = lax.fori_loop(0, nx, layer_three, (zero, zero, zero), unroll=UNROLL)
    row = lax.broadcasted_iota(jnp.int32, (8, depth), 0)
    tile = jnp.zeros((8, depth), F32)
    for i, s in enumerate(sums):
        tile = jnp.where(row == i, jnp.sum(s, axis=0, keepdims=True), tile)
    folded = tile[:, 0:128]
    for i in range(1, depth // 128):
        folded = folded + tile[:, 128 * i : 128 * i + 128]

    def reduce_over(value, slot, slots, me, n, sends, recvs, peer_id):
        part[slot] = value
        slots[me] = value
        todo = []
        for i in range(1, n):
            c = pltpu.make_async_remote_copy(
                src_ref=part.at[slot],
                dst_ref=slots.at[me],
                send_sem=sends.at[i],
                recv_sem=recvs.at[i],
                device_id=peer_id(lax.rem(me + i, n)),
                device_id_type=MESH,
            )
            c.start()
            todo.append(c)
        for i, c in enumerate(todo):
            back = pltpu.make_async_remote_copy(
                src_ref=part.at[slot],
                dst_ref=slots.at[lax.rem(me + n - (i + 1), n)],
                send_sem=sends.at[i + 1],
                recv_sem=recvs.at[i + 1],
                device_id=peer_id(lax.rem(me + i + 1, n)),
                device_id_type=MESH,
            )
            back.wait_recv()
        total = slots[0]
        for i in range(1, n):
            total = total + slots[i]
        return total, todo

    over_y, todo_y = reduce_over(folded, 0, red_y, gy, n_gy, ry_send, ry_recv, lambda j: (gx, j))
    total, todo_x = reduce_over(over_y, 1, red_x, gx, n_gx, rx_send, rx_recv, lambda j: (j, gy))
    sums = jnp.sum(total, axis=1, keepdims=True)
    damping = 8.0 * float(nx * n_gx * ny * n_gy * depth)
    scale = sums[1:2] / (sums[0:1] + sums[2:3] + damping)

    def finish(p, carry):
        out_step[p] = scale * out_step[p]
        return carry

    lax.fori_loop(0, nx, finish, 0, unroll=4)
    for group in (copies_a, copies_b, copies_g):
        for c in group:
            c.sent()
    for c in todo_y + todo_x:
        c.wait_send()


def slabs(weight, slots):
    _, c, d = weight.shape
    w = weight.astype(F32).reshape(3, 9, c, d).transpose(1, 3, 0, 2)
    w = jnp.broadcast_to(w[:, :, :, None, :], (9, d, 3, slots, c))
    return w.reshape(9, d, 3 * slots * c)


def shards(n_gx, n_gy, speed, before, now, src, prior, w_first, b_first, w_mid, b_mid, w_last):
    nx, ny, depth = now.shape
    out = jax.ShapeDtypeStruct(now.shape, F32)
    vmem = pl.BlockSpec(memory_space=pltpu.VMEM)
    half, groups = nx // 2, nx // 4
    r1, r2 = ny + 4, ny + 2
    ch = b_first.shape[0]
    return pl.pallas_call(
        functools.partial(kernel, n_gx, n_gy),
        out_shape=(out,) * 4,
        in_specs=[vmem] * 10,
        out_specs=(vmem,) * 4,
        scratch_shapes=[
            pltpu.VMEM((nx + 8, ny + 16, depth), F32),
            pltpu.VMEM((nx + 8, ny + 16, depth), F32),
            pltpu.VMEM((2, half, 8, depth), F32),
            pltpu.VMEM((2, half, 8, depth), F32),
            pltpu.VMEM((2, half, 8, depth), F32),
            pltpu.VMEM((2, half, 8, depth), F32),
            pltpu.VMEM((nx + 8, 2 * ny, depth), BF16),
            pltpu.VMEM((2, groups, 16, depth), BF16),
            pltpu.VMEM((2, groups + 2, 16, depth), BF16),
            pltpu.VMEM((nx + 4, r1 * ch, depth), BF16),
            pltpu.VMEM((nx + 2, r2 * ch, depth), BF16),
            pltpu.VMEM((3 * r1 * ch, 6 * ny), BF16),
            pltpu.VMEM((3 * r2 * ch, 3 * r1 * ch), BF16),
            pltpu.VMEM((3 * ny, 3 * r2 * ch), BF16),
            pltpu.VMEM((2, 8, 128), F32),
            pltpu.VMEM((n_gy, 8, 128), F32),
            pltpu.VMEM((n_gx, 8, 128), F32),
            pltpu.SemaphoreType.DMA((16,)),
            pltpu.SemaphoreType.DMA((16,)),
            pltpu.SemaphoreType.DMA((n_gy,)),
            pltpu.SemaphoreType.DMA((n_gy,)),
            pltpu.SemaphoreType.DMA((n_gx,)),
            pltpu.SemaphoreType.DMA((n_gx,)),
        ],
        compiler_params=pltpu.CompilerParams(
            collective_id=0, has_side_effects=True, vmem_limit_bytes=40 * 1024 * 1024
        ),
    )(
        speed,
        before,
        now,
        src,
        prior,
        slabs(w_first, 2 * ny),
        w_mid.reshape(3, 9, ch, ch).transpose(1, 3, 0, 2).reshape(9 * ch, 3 * ch),
        slabs(w_last, r2),
        b_first.reshape(ch, 1),
        b_mid.reshape(ch, 1),
    )


def solution(mesh):
    brick = P("gx", "gy", None)
    return jax.shard_map(
        functools.partial(shards, mesh.shape["gx"], mesh.shape["gy"]),
        mesh=mesh,
        in_specs=(brick, brick, brick, P(None, "gx", "gy", None), brick, P(), P(), P(), P(), P()),
        out_specs=(brick,) * 4,
        check_vma=False,
    )
```

```python
import functools

import jax
import jax.numpy as jnp
from jax import lax
from jax.experimental import pallas as pl
from jax.experimental.pallas import tpu as pltpu
from jax.sharding import PartitionSpec as P

COEFS = (-205.0 / 72.0, 8.0 / 5.0, -1.0 / 5.0, 8.0 / 315.0, -1.0 / 560.0)
MESH = pl.DeviceIdType.MESH
F32 = jnp.float32
BF16 = jnp.bfloat16
UNROLL = True
WAVE_UNROLL = 4


def shift_z(v, k):
    depth = v.shape[-1]
    lane = lax.broadcasted_iota(jnp.int32, v.shape, v.ndim - 1)
    rolled = pltpu.roll(v, (-k) % depth, v.ndim - 1)
    return jnp.where((lane + k >= 0) & (lane + k < depth), rolled, 0.0)


def laplace_z(center):
    total = 3.0 * COEFS[0] * center
    for k in range(1, 5):
        total = total + COEFS[k] * (shift_z(center, k) + shift_z(center, -k))
    return total


def laplace_xy(ext, x, ny):
    total = None
    for k in range(1, 5):
        cycle = ext[x + 4 + k, 8 : 8 + ny, :] + ext[x + 4 - k, 8 : 8 + ny, :]
        cycle = cycle + ext[x + 4, 8 + k : 8 + k + ny, :]
        cycle = cycle + ext[x + 4, 8 - k : 8 - k + ny, :]
        total = COEFS[k] * cycle if total is None else total + COEFS[k] * cycle
    return total


def kernel(
    n_gx,
    n_gy,
    speed_hbm,
    before_hbm,
    now_hbm,
    src_hbm,
    prior_hbm,
    raw,
    raw_b1,
    raw_b2,
    out_next,
    out_after,
    out_grad,
    out_step,
    speed,
    before,
    src,
    prior,
    load_sem,
    ext_a,
    ext_b,
    pack_a,
    pack_b,
    recv_a,
    recv_b,
    grad,
    pack_g,
    recv_g,
    h1,
    h2,
    w1,
    w2,
    w3,
    part,
    red_y,
    red_x,
    send_sem,
    recv_sem,
    ry_send,
    ry_recv,
    rx_send,
    rx_recv,
):
    nx, ny, depth = now_hbm.shape
    gx, gy = lax.axis_index("gx"), lax.axis_index("gy")
    barrier = pltpu.get_barrier_semaphore()
    own = pl.ds(8, ny)
    loads = [
        pltpu.make_async_copy(source, target, load_sem.at[i])
        for i, (source, target) in enumerate(
            (
                (now_hbm, ext_a.at[pl.ds(4, nx), own, :]),
                (before_hbm, before),
                (speed_hbm, speed),
                (src_hbm, src),
                (prior_hbm, prior),
            )
        )
    ]
    for load in loads:
        load.start()

    def there(dx, dy):
        ok = None
        for pos, d, n in ((gx, dx, n_gx), (gy, dy, n_gy)):
            if d:
                one = (pos + d >= 0) & (pos + d < n)
                ok = one if ok is None else ok & one
        return ok

    for i in range(1, n_gy):
        pl.semaphore_signal(
            barrier, inc=1, device_id=(gx, lax.rem(gy + i, n_gy)), device_id_type=MESH
        )
    for i in range(1, n_gx):
        pl.semaphore_signal(
            barrier, inc=1, device_id=(lax.rem(gx + i, n_gx), gy), device_id_type=MESH
        )
    diagonals = ((-1, -1), (-1, 1), (1, -1), (1, 1))
    for dx, dy in diagonals:

        @pl.when(there(dx, dy))
        def _(dx=dx, dy=dy):
            pl.semaphore_signal(barrier, inc=1, device_id=(gx + dx, gy + dy), device_id_type=MESH)

    class Copy:
        def __init__(self, ident, source, target, dx, dy):
            self.make = lambda: pltpu.make_async_remote_copy(
                src_ref=source,
                dst_ref=target,
                send_sem=send_sem.at[ident],
                recv_sem=recv_sem.at[ident],
                device_id=(gx + dx, gy + dy),
                device_id_type=MESH,
            )
            self.to = there(dx, dy)
            self.origin = there(-dx, -dy)
            self.target = target

        def start(self):
            @pl.when(self.to)
            def _():
                self.make().start()

        def clear(self):
            @pl.when(jnp.logical_not(self.origin))
            def _():
                self.target[...] = jnp.zeros(self.target.shape, self.target.dtype)

        def arrive(self):
            @pl.when(self.origin)
            def _():
                self.make().wait_recv()

        def sent(self):
            @pl.when(self.to)
            def _():
                self.make().wait_send()

    def wave_copies(base, ext, pack, recv):
        return (
            Copy(base, ext.at[pl.ds(nx, 4), own, :], ext.at[pl.ds(0, 4), own, :], 1, 0),
            Copy(base + 1, ext.at[pl.ds(4, 4), own, :], ext.at[pl.ds(nx + 4, 4), own, :], -1, 0),
            Copy(base + 2, pack.at[1], recv.at[0], 0, 1),
            Copy(base + 3, pack.at[0], recv.at[1], 0, -1),
        )

    copies_a = wave_copies(0, ext_a, pack_a, recv_a)
    copies_b = wave_copies(4, ext_b, pack_b, recv_b)
    row16 = pl.ds(0, ny)
    groups = nx // 4
    mid = pl.ds(1, groups)
    copies_g = (
        Copy(8, grad.at[pl.ds(nx, 4), row16, :], grad.at[pl.ds(0, 4), row16, :], 1, 0),
        Copy(9, grad.at[pl.ds(4, 4), row16, :], grad.at[pl.ds(nx + 4, 4), row16, :], -1, 0),
        Copy(10, pack_g.at[1], recv_g.at[0, mid], 0, 1),
        Copy(11, pack_g.at[0], recv_g.at[1, mid], 0, -1),
        Copy(12, pack_g.at[1, groups - 1], recv_g.at[0, 0], 1, 1),
        Copy(13, pack_g.at[1, 0], recv_g.at[0, groups + 1], -1, 1),
        Copy(14, pack_g.at[0, groups - 1], recv_g.at[1, 0], 1, -1),
        Copy(15, pack_g.at[0, 0], recv_g.at[1, groups + 1], -1, -1),
    )

    def pack_wave(ext, pack):
        half = nx // 2
        for i in range(half):
            for side, at in ((0, 8), (1, 8 + ny - 4)):
                pack[side, i] = jnp.concatenate(
                    [ext[4 + i, at : at + 4, :], ext[4 + half + i, at : at + 4, :]], axis=0
                )

    def unpack_wave(ext, recv):
        half = nx // 2
        for i in range(half):
            for side, at in ((0, 4), (1, 8 + ny)):
                tile = recv[side, i]
                ext[4 + i, at : at + 4, :] = tile[0:4]
                ext[4 + half + i, at : at + 4, :] = tile[4:8]

    loads[0].wait()
    pack_wave(ext_a, pack_a)
    for group in (copies_a, copies_b, copies_g):
        for c in group:
            c.clear()

    wanted = (n_gy - 1) + (n_gx - 1)
    for dx, dy in diagonals:
        wanted = wanted + there(dx, dy).astype(jnp.int32)
    pl.semaphore_wait(barrier, wanted)
    for c in copies_a:
        c.start()

    def band(out, slabs, e, rows, per_row, first_out, width, place):
        shape = (rows * per_row, 3 * width)
        col = lax.broadcasted_iota(jnp.int32, shape, 1)
        row = lax.broadcasted_iota(jnp.int32, shape, 0)
        slot = col - jnp.where(col >= width, width, 0) - jnp.where(col >= 2 * width, width, 0)
        y_out = (row >> 3 if per_row == 8 else row) + first_out
        gap = place(slot) - y_out
        total = jnp.zeros(shape, F32)
        for b in range(3):
            slab = slabs[3 * b + e]
            if per_row == 8:
                full = jnp.concatenate([slab] * rows, axis=0)
            else:
                full = jnp.broadcast_to(slab, shape)
            total = jnp.where(gap == b - 1, full, total)
        out[e * shape[0] : (e + 1) * shape[0], :] = total.astype(BF16)

    def grad_slot(slot):
        return jnp.where(
            slot < ny, slot, jnp.where(slot < ny + 4, slot - ny - 4, jnp.where(slot < ny + 8, slot - 4, 999))
        )

    r1, r2 = ny + 4, ny + 2
    m1, m2 = 8 * r1, 8 * r2
    def third(index, size):
        return jnp.where(index >= size, 1, 0) + jnp.where(index >= 2 * size, 1, 0)

    def iota(shape, dim):
        return lax.broadcasted_iota(jnp.int32, shape, dim)

    def turned(rows):
        eye = jnp.where(iota((8, 8), 0) == iota((8, 8), 1), 1.0, 0.0).astype(BF16)
        return lax.dot_general(
            eye, rows.astype(BF16), (((1,), (1,)), ((), ())), preferred_element_type=F32
        )

    def stacked(flat, step):
        tall = jnp.concatenate([flat] * 9, axis=0)
        tap = iota(tall.shape, 1) >> step
        return jnp.where(tap - 9 * third(tap, 9) == iota(tall.shape, 0) >> 3, tall, 0.0).astype(BF16)

    def matches(count, step, width):
        shape = (count, 3 * width)
        tap, col = iota(shape, 0), iota(shape, 1)
        hit = third(tap >> step, 9) == third(col, width)
        return hit & ((tap & 7) == (col & 7)) if step else hit

    def one_hot(hit):
        return jnp.where(hit, 1.0, 0.0).astype(BF16)

    def column(bias):
        wide = jnp.broadcast_to(bias[...], (8, 8))
        return jnp.sum(jnp.where(iota((8, 8), 0) == iota((8, 8), 1), wide, 0.0), axis=1, keepdims=True)

    b1, b2 = column(raw_b1), column(raw_b2)
    rows = jnp.concatenate([raw[k].astype(F32) for k in range(27)], axis=0)
    wide2 = jnp.dot(
        stacked(turned(rows[:, 0:8]), 3), one_hot(matches(216, 3, m1)), preferred_element_type=F32
    )
    tap = iota((16, 216), 1) >> 3
    own_tap = one_hot(tap - 9 * third(tap, 9) == iota((16, 216), 0))
    wide3 = jnp.dot(
        own_tap,
        jnp.where(matches(216, 3, m2), rows[:, 8:9], 0.0).astype(BF16),
        preferred_element_type=F32,
    )
    tap = iota((72, 216), 1) >> 3
    own_row = (tap - 9 * third(tap, 9)) * 8 + (iota((72, 216), 1) & 7) == iota((72, 216), 0)
    same_a = third(iota((216, 6 * ny), 0) >> 3, 9) == third(iota((216, 6 * ny), 1), 2 * ny)
    wide1 = jnp.dot(
        one_hot(own_row),
        jnp.where(same_a, rows[:, 9:10], 0.0).astype(BF16),
        preferred_element_type=F32,
    )
    s1 = [wide1[8 * k : 8 * k + 8] for k in range(9)]
    s2 = [wide2[8 * k : 8 * k + 8] for k in range(9)]
    s3 = [wide3[k : k + 1] for k in range(9)]
    for e in range(3):
        band(w1, s1, e, r1, 8, -2, 2 * ny, grad_slot)
        band(w2, s2, e, r2, 8, -1, r1 * 8, lambda s: (s >> 3) - 2)
        band(w3, s3, e, ny, 1, 0, r2 * 8, lambda s: (s >> 3) - 1)

    for load in loads[1:]:
        load.wait()

    def inner_one(x, carry):
        center = ext_a[x + 4, 8 : 8 + ny, :]
        out_next[x] = 2.0 * center - before[x] + speed[x] * laplace_z(center)
        return carry

    lax.fori_loop(0, nx, inner_one, 0, unroll=WAVE_UNROLL)
    for c in copies_a:
        c.arrive()
    unpack_wave(ext_a, recv_a)

    def step_one(x, carry):
        value = out_next[x] + speed[x] * laplace_xy(ext_a, x, ny)
        out_next[x] = value
        ext_b[x + 4, 8 : 8 + ny, :] = value
        return carry

    lax.fori_loop(0, nx, step_one, 0, unroll=WAVE_UNROLL)
    pack_wave(ext_b, pack_b)
    for c in copies_b:
        c.start()

    def inner_two(x, carry):
        center = out_next[x]
        out_after[x] = 2.0 * center - ext_a[x + 4, 8 : 8 + ny, :] + speed[x] * laplace_z(center)
        return carry

    lax.fori_loop(0, nx, inner_two, 0, unroll=WAVE_UNROLL)
    for c in copies_b:
        c.arrive()
    unpack_wave(ext_b, recv_b)

    def step_two(x, carry):
        center = out_next[x]
        value = out_after[x] + speed[x] * laplace_xy(ext_b, x, ny)
        out_after[x] = value
        gradient = prior[x] + src[0, x] * center + src[1, x] * value
        out_grad[x] = gradient
        grad[x + 4, 0:ny, :] = gradient.astype(BF16)
        return carry

    lax.fori_loop(0, nx, step_two, 0, unroll=WAVE_UNROLL)
    for t in range(groups):
        for side, at in ((0, 0), (1, ny - 4)):
            pack_g[side, t] = jnp.concatenate(
                [out_grad[4 * t + j, at : at + 4, :] for j in range(4)], axis=0
            ).astype(BF16)
    for c in copies_g:
        c.start()
    for c in copies_g:
        c.arrive()
    for t in range(groups + 2):
        low = recv_g[0, t].astype(F32)
        high = recv_g[1, t].astype(F32)
        for j in range(4):
            grad[4 * t + j, ny : 2 * ny, :] = jnp.concatenate(
                [low[4 * j : 4 * j + 4], high[4 * j : 4 * j + 4], jnp.zeros((ny - 8, depth), F32)],
                axis=0,
            ).astype(BF16)

    x_min = jnp.where(gx == 0, 0, -8)
    x_max = jnp.where(gx == n_gx - 1, nx, nx + 8)
    y_min = jnp.where(gy == 0, 0, -8)
    y_max = jnp.where(gy == n_gy - 1, ny, ny + 8)

    def conv_plane(weight, rhs, rows):
        res = jnp.dot(weight[...], rhs, preferred_element_type=F32)
        return (
            res[rows : 2 * rows] + shift_z(res[:rows], -1) + shift_z(res[2 * rows :], 1)
        )

    def hidden(value, bias, rows, first, x):
        y = (lax.broadcasted_iota(jnp.int32, value.shape, 0) >> 3) + first
        inside = (y >= y_min) & (y < y_max) & (x >= x_min) & (x < x_max)
        full = jnp.concatenate([jnp.broadcast_to(bias, (8, depth))] * rows, axis=0)
        return jnp.where(inside, jnp.maximum(value + full, 0.0), 0.0).astype(BF16)

    def layer_one(p, carry):
        rhs = grad[pl.ds(p + 1, 3)].reshape(6 * ny, depth)
        h1[p] = hidden(conv_plane(w1, rhs, m1), b1, r1, -2, p - 2)
        return carry

    lax.fori_loop(0, nx + 4, layer_one, 0, unroll=UNROLL)

    def layer_two(p, carry):
        rhs = h1[pl.ds(p, 3)].reshape(3 * m1, depth)
        h2[p] = hidden(conv_plane(w2, rhs, m2), b2, r2, -1, p - 1)
        return carry

    lax.fori_loop(0, nx + 2, layer_two, 0, unroll=UNROLL)

    zero = jnp.zeros((ny, depth), F32)

    def layer_three(p, carry):
        gg, gd, dd = carry
        rhs = h2[pl.ds(p, 3)].reshape(3 * m2, depth)
        g = out_grad[p]
        d = conv_plane(w3, rhs, ny) + g
        out_step[p] = d
        return gg + g * g, gd + g * d, dd + d * d

    sums = lax.fori_loop(0, nx, layer_three, (zero, zero, zero), unroll=UNROLL)
    row = lax.broadcasted_iota(jnp.int32, (8, depth), 0)
    tile = jnp.zeros((8, depth), F32)
    for i, s in enumerate(sums):
        tile = jnp.where(row == i, jnp.sum(s, axis=0, keepdims=True), tile)
    folded = tile[:, 0:128]
    for i in range(1, depth // 128):
        folded = folded + tile[:, 128 * i : 128 * i + 128]

    def reduce_over(value, slot, slots, me, n, sends, recvs, peer_id):
        part[slot] = value
        slots[me] = value
        todo = []
        for i in range(1, n):
            c = pltpu.make_async_remote_copy(
                src_ref=part.at[slot],
                dst_ref=slots.at[me],
                send_sem=sends.at[i],
                recv_sem=recvs.at[i],
                device_id=peer_id(lax.rem(me + i, n)),
                device_id_type=MESH,
            )
            c.start()
            todo.append(c)
        for i, c in enumerate(todo):
            back = pltpu.make_async_remote_copy(
                src_ref=part.at[slot],
                dst_ref=slots.at[lax.rem(me + n - (i + 1), n)],
                send_sem=sends.at[i + 1],
                recv_sem=recvs.at[i + 1],
                device_id=peer_id(lax.rem(me + i + 1, n)),
                device_id_type=MESH,
            )
            back.wait_recv()
        total = slots[0]
        for i in range(1, n):
            total = total + slots[i]
        return total, todo

    over_y, todo_y = reduce_over(folded, 0, red_y, gy, n_gy, ry_send, ry_recv, lambda j: (gx, j))
    total, todo_x = reduce_over(over_y, 1, red_x, gx, n_gx, rx_send, rx_recv, lambda j: (j, gy))
    sums = jnp.sum(total, axis=1, keepdims=True)
    damping = 8.0 * float(nx * n_gx * ny * n_gy * depth)
    scale = sums[1:2] / (sums[0:1] + sums[2:3] + damping)

    def finish(p, carry):
        out_step[p] = scale * out_step[p]
        return carry

    lax.fori_loop(0, nx, finish, 0, unroll=4)
    for group in (copies_a, copies_b, copies_g):
        for c in group:
            c.sent()
    for c in todo_y + todo_x:
        c.wait_send()


def hand_on(*refs):
    for source, target in zip(refs[:4], refs[4:]):
        target[...] = source[...]


def shards(n_gx, n_gy, speed, before, now, src, prior, w_first, b_first, w_mid, b_mid, w_last):
    nx, ny, depth = now.shape
    out = jax.ShapeDtypeStruct(now.shape, F32)
    vmem = pl.BlockSpec(memory_space=pltpu.VMEM)
    half, groups = nx // 2, nx // 4
    r1, r2 = ny + 4, ny + 2
    ch = b_first.shape[0]
    outs = pl.pallas_call(
        functools.partial(kernel, n_gx, n_gy),
        out_shape=(out,) * 4,
        in_specs=[pl.BlockSpec(memory_space=pl.ANY)] * 5 + [vmem] * 3,
        out_specs=(vmem,) * 4,
        scratch_shapes=[
            pltpu.VMEM(now.shape, F32),
            pltpu.VMEM(now.shape, F32),
            pltpu.VMEM(src.shape, F32),
            pltpu.VMEM(now.shape, F32),
            pltpu.SemaphoreType.DMA((5,)),
            pltpu.VMEM((nx + 8, ny + 16, depth), F32),
            pltpu.VMEM((nx + 8, ny + 16, depth), F32),
            pltpu.VMEM((2, half, 8, depth), F32),
            pltpu.VMEM((2, half, 8, depth), F32),
            pltpu.VMEM((2, half, 8, depth), F32),
            pltpu.VMEM((2, half, 8, depth), F32),
            pltpu.VMEM((nx + 8, 2 * ny, depth), BF16),
            pltpu.VMEM((2, groups, 16, depth), BF16),
            pltpu.VMEM((2, groups + 2, 16, depth), BF16),
            pltpu.VMEM((nx + 4, r1 * ch, depth), BF16),
            pltpu.VMEM((nx + 2, r2 * ch, depth), BF16),
            pltpu.VMEM((3 * r1 * ch, 6 * ny), BF16),
            pltpu.VMEM((3 * r2 * ch, 3 * r1 * ch), BF16),
            pltpu.VMEM((3 * ny, 3 * r2 * ch), BF16),
            pltpu.VMEM((2, 8, 128), F32),
            pltpu.VMEM((n_gy, 8, 128), F32),
            pltpu.VMEM((n_gx, 8, 128), F32),
            pltpu.SemaphoreType.DMA((16,)),
            pltpu.SemaphoreType.DMA((16,)),
            pltpu.SemaphoreType.DMA((n_gy,)),
            pltpu.SemaphoreType.DMA((n_gy,)),
            pltpu.SemaphoreType.DMA((n_gx,)),
            pltpu.SemaphoreType.DMA((n_gx,)),
        ],
        compiler_params=pltpu.CompilerParams(
            collective_id=0, has_side_effects=True, vmem_limit_bytes=60 * 1024 * 1024
        ),
    )(
        speed,
        before,
        now,
        src,
        prior,
        jnp.concatenate([w_mid, w_last, w_first.reshape(27, ch, 1)], axis=2),
        b_first.reshape(1, ch),
        b_mid.reshape(1, ch),
    )
    block = pl.BlockSpec((nx // 4, ny, depth), lambda i: (i, 0, 0))
    return pl.pallas_call(
        hand_on,
        grid=(4,),
        out_shape=(out,) * 4,
        in_specs=[block] * 4,
        out_specs=(block,) * 4,
    )(*outs)


def solution(mesh):
    brick = P("gx", "gy", None)
    return jax.shard_map(
        functools.partial(shards, mesh.shape["gx"], mesh.shape["gy"]),
        mesh=mesh,
        in_specs=(brick, brick, brick, P(None, "gx", "gy", None), brick, P(), P(), P(), P(), P()),
        out_specs=(brick,) * 4,
        check_vma=False,
    )
```

```python
import functools

import jax
import jax.numpy as jnp
from jax import lax
from jax.experimental import pallas as pl
from jax.experimental.pallas import tpu as pltpu
from jax.sharding import PartitionSpec as P

COEFS = (-205.0 / 72.0, 8.0 / 5.0, -1.0 / 5.0, 8.0 / 315.0, -1.0 / 560.0)
MESH = pl.DeviceIdType.MESH
F32 = jnp.float32
BF16 = jnp.bfloat16
UNROLL = True
WAVE_UNROLL = 8


def shift_z(v, k):
    depth = v.shape[-1]
    lane = lax.broadcasted_iota(jnp.int32, v.shape, v.ndim - 1)
    rolled = pltpu.roll(v, (-k) % depth, v.ndim - 1)
    return jnp.where((lane + k >= 0) & (lane + k < depth), rolled, 0.0)


def laplace_z(center):
    total = 3.0 * COEFS[0] * center
    for k in range(1, 5):
        total = total + COEFS[k] * (shift_z(center, k) + shift_z(center, -k))
    return total


def laplace_xy(ext, x, ny):
    total = None
    for k in range(1, 5):
        cycle = ext[x + 4 + k, 8 : 8 + ny, :] + ext[x + 4 - k, 8 : 8 + ny, :]
        cycle = cycle + ext[x + 4, 8 + k : 8 + k + ny, :]
        cycle = cycle + ext[x + 4, 8 - k : 8 - k + ny, :]
        total = COEFS[k] * cycle if total is None else total + COEFS[k] * cycle
    return total


def kernel(
    n_gx,
    n_gy,
    speed_hbm,
    before_hbm,
    now_hbm,
    src_hbm,
    prior_hbm,
    raw,
    raw_b1,
    raw_b2,
    out_next,
    out_after,
    out_grad,
    out_step,
    speed,
    before,
    src,
    prior,
    load_sem,
    ext_a,
    ext_b,
    pack_a,
    pack_b,
    recv_a,
    recv_b,
    grad,
    pack_g,
    recv_g,
    h1,
    h2,
    w1,
    w2,
    w3,
    part,
    red_y,
    red_x,
    send_sem,
    recv_sem,
    ry_send,
    ry_recv,
    rx_send,
    rx_recv,
):
    nx, ny, depth = now_hbm.shape
    gx, gy = lax.axis_index("gx"), lax.axis_index("gy")
    barrier = pltpu.get_barrier_semaphore()
    own = pl.ds(8, ny)
    loads = [
        pltpu.make_async_copy(source, target, load_sem.at[i])
        for i, (source, target) in enumerate(
            (
                (now_hbm, ext_a.at[pl.ds(4, nx), own, :]),
                (before_hbm, before),
                (speed_hbm, speed),
                (src_hbm, src),
                (prior_hbm, prior),
            )
        )
    ]
    for load in loads:
        load.start()

    def there(dx, dy):
        ok = None
        for pos, d, n in ((gx, dx, n_gx), (gy, dy, n_gy)):
            if d:
                one = (pos + d >= 0) & (pos + d < n)
                ok = one if ok is None else ok & one
        return ok

    for i in range(1, n_gy):
        pl.semaphore_signal(
            barrier, inc=1, device_id=(gx, lax.rem(gy + i, n_gy)), device_id_type=MESH
        )
    for i in range(1, n_gx):
        pl.semaphore_signal(
            barrier, inc=1, device_id=(lax.rem(gx + i, n_gx), gy), device_id_type=MESH
        )
    diagonals = ((-1, -1), (-1, 1), (1, -1), (1, 1))
    for dx, dy in diagonals:

        @pl.when(there(dx, dy))
        def _(dx=dx, dy=dy):
            pl.semaphore_signal(barrier, inc=1, device_id=(gx + dx, gy + dy), device_id_type=MESH)

    class Copy:
        def __init__(self, ident, source, target, dx, dy):
            self.make = lambda: pltpu.make_async_remote_copy(
                src_ref=source,
                dst_ref=target,
                send_sem=send_sem.at[ident],
                recv_sem=recv_sem.at[ident],
                device_id=(gx + dx, gy + dy),
                device_id_type=MESH,
            )
            self.to = there(dx, dy)
            self.origin = there(-dx, -dy)
            self.target = target

        def start(self):
            @pl.when(self.to)
            def _():
                self.make().start()

        def clear(self):
            @pl.when(jnp.logical_not(self.origin))
            def _():
                self.target[...] = jnp.zeros(self.target.shape, self.target.dtype)

        def arrive(self):
            @pl.when(self.origin)
            def _():
                self.make().wait_recv()

        def sent(self):
            @pl.when(self.to)
            def _():
                self.make().wait_send()

    def wave_copies(base, ext, pack, recv):
        return (
            Copy(base, ext.at[pl.ds(nx, 4), own, :], ext.at[pl.ds(0, 4), own, :], 1, 0),
            Copy(base + 1, ext.at[pl.ds(4, 4), own, :], ext.at[pl.ds(nx + 4, 4), own, :], -1, 0),
            Copy(base + 2, pack.at[1], recv.at[0], 0, 1),
            Copy(base + 3, pack.at[0], recv.at[1], 0, -1),
        )

    copies_a = wave_copies(0, ext_a, pack_a, recv_a)
    copies_b = wave_copies(4, ext_b, pack_b, recv_b)
    row16 = pl.ds(0, ny)
    groups = nx // 4
    mid = pl.ds(1, groups)
    copies_g = (
        Copy(8, grad.at[pl.ds(nx, 4), row16, :], grad.at[pl.ds(0, 4), row16, :], 1, 0),
        Copy(9, grad.at[pl.ds(4, 4), row16, :], grad.at[pl.ds(nx + 4, 4), row16, :], -1, 0),
        Copy(10, pack_g.at[1], recv_g.at[0, mid], 0, 1),
        Copy(11, pack_g.at[0], recv_g.at[1, mid], 0, -1),
        Copy(12, pack_g.at[1, groups - 1], recv_g.at[0, 0], 1, 1),
        Copy(13, pack_g.at[1, 0], recv_g.at[0, groups + 1], -1, 1),
        Copy(14, pack_g.at[0, groups - 1], recv_g.at[1, 0], 1, -1),
        Copy(15, pack_g.at[0, 0], recv_g.at[1, groups + 1], -1, -1),
    )

    def pack_wave(ext, pack):
        half = nx // 2
        for i in range(half):
            for side, at in ((0, 8), (1, 8 + ny - 4)):
                pack[side, i] = jnp.concatenate(
                    [ext[4 + i, at : at + 4, :], ext[4 + half + i, at : at + 4, :]], axis=0
                )

    def unpack_wave(ext, recv):
        half = nx // 2
        for i in range(half):
            for side, at in ((0, 4), (1, 8 + ny)):
                tile = recv[side, i]
                ext[4 + i, at : at + 4, :] = tile[0:4]
                ext[4 + half + i, at : at + 4, :] = tile[4:8]

    loads[0].wait()
    pack_wave(ext_a, pack_a)
    for group in (copies_a, copies_b, copies_g):
        for c in group:
            c.clear()

    wanted = (n_gy - 1) + (n_gx - 1)
    for dx, dy in diagonals:
        wanted = wanted + there(dx, dy).astype(jnp.int32)
    pl.semaphore_wait(barrier, wanted)
    for c in copies_a:
        c.start()

    def band(out, slabs, e, rows, per_row, first_out, width, place):
        shape = (rows * per_row, 3 * width)
        col = lax.broadcasted_iota(jnp.int32, shape, 1)
        row = lax.broadcasted_iota(jnp.int32, shape, 0)
        slot = col - jnp.where(col >= width, width, 0) - jnp.where(col >= 2 * width, width, 0)
        y_out = (row >> 3 if per_row == 8 else row) + first_out
        gap = place(slot) - y_out
        total = jnp.zeros(shape, F32)
        for b in range(3):
            slab = slabs[3 * b + e]
            if per_row == 8:
                full = jnp.concatenate([slab] * rows, axis=0)
            else:
                full = jnp.broadcast_to(slab, shape)
            total = jnp.where(gap == b - 1, full, total)
        out[e * shape[0] : (e + 1) * shape[0], :] = total.astype(BF16)

    def grad_slot(slot):
        return jnp.where(
            slot < ny, slot, jnp.where(slot < ny + 4, slot - ny - 4, jnp.where(slot < ny + 8, slot - 4, 999))
        )

    r1, r2 = ny + 4, ny + 2
    m1, m2 = 8 * r1, 8 * r2
    def third(index, size):
        return jnp.where(index >= size, 1, 0) + jnp.where(index >= 2 * size, 1, 0)

    def iota(shape, dim):
        return lax.broadcasted_iota(jnp.int32, shape, dim)

    def turned(rows):
        eye = jnp.where(iota((8, 8), 0) == iota((8, 8), 1), 1.0, 0.0).astype(BF16)
        return lax.dot_general(
            eye, rows.astype(BF16), (((1,), (1,)), ((), ())), preferred_element_type=F32
        )

    def stacked(flat, step):
        tall = jnp.concatenate([flat] * 9, axis=0)
        tap = iota(tall.shape, 1) >> step
        return jnp.where(tap - 9 * third(tap, 9) == iota(tall.shape, 0) >> 3, tall, 0.0).astype(BF16)

    def matches(count, step, width):
        shape = (count, 3 * width)
        tap, col = iota(shape, 0), iota(shape, 1)
        hit = third(tap >> step, 9) == third(col, width)
        return hit & ((tap & 7) == (col & 7)) if step else hit

    def one_hot(hit):
        return jnp.where(hit, 1.0, 0.0).astype(BF16)

    def column(bias):
        wide = jnp.broadcast_to(bias[...], (8, 8))
        return jnp.sum(jnp.where(iota((8, 8), 0) == iota((8, 8), 1), wide, 0.0), axis=1, keepdims=True)

    b1, b2 = column(raw_b1), column(raw_b2)
    rows = jnp.concatenate([raw[k].astype(F32) for k in range(27)], axis=0)
    wide2 = jnp.dot(
        stacked(turned(rows[:, 0:8]), 3), one_hot(matches(216, 3, m1)), preferred_element_type=F32
    )
    tap = iota((16, 216), 1) >> 3
    own_tap = one_hot(tap - 9 * third(tap, 9) == iota((16, 216), 0))
    wide3 = jnp.dot(
        own_tap,
        jnp.where(matches(216, 3, m2), rows[:, 8:9], 0.0).astype(BF16),
        preferred_element_type=F32,
    )
    tap = iota((72, 216), 1) >> 3
    own_row = (tap - 9 * third(tap, 9)) * 8 + (iota((72, 216), 1) & 7) == iota((72, 216), 0)
    same_a = third(iota((216, 6 * ny), 0) >> 3, 9) == third(iota((216, 6 * ny), 1), 2 * ny)
    wide1 = jnp.dot(
        one_hot(own_row),
        jnp.where(same_a, rows[:, 9:10], 0.0).astype(BF16),
        preferred_element_type=F32,
    )
    s1 = [wide1[8 * k : 8 * k + 8] for k in range(9)]
    s2 = [wide2[8 * k : 8 * k + 8] for k in range(9)]
    s3 = [wide3[k : k + 1] for k in range(9)]
    for e in range(3):
        band(w1, s1, e, r1, 8, -2, 2 * ny, grad_slot)
        band(w2, s2, e, r2, 8, -1, r1 * 8, lambda s: (s >> 3) - 2)
        band(w3, s3, e, ny, 1, 0, r2 * 8, lambda s: (s >> 3) - 1)

    for load in loads[1:]:
        load.wait()

    def inner_one(x, carry):
        center = ext_a[x + 4, 8 : 8 + ny, :]
        out_next[x] = 2.0 * center - before[x] + speed[x] * laplace_z(center)
        return carry

    lax.fori_loop(0, nx, inner_one, 0, unroll=WAVE_UNROLL)
    for c in copies_a:
        c.arrive()
    unpack_wave(ext_a, recv_a)

    def step_one(x, carry):
        value = out_next[x] + speed[x] * laplace_xy(ext_a, x, ny)
        out_next[x] = value
        ext_b[x + 4, 8 : 8 + ny, :] = value
        return carry

    lax.fori_loop(0, nx, step_one, 0, unroll=WAVE_UNROLL)
    for c in copies_b[:2]:
        c.start()
    pack_wave(ext_b, pack_b)
    for c in copies_b[2:]:
        c.start()

    def inner_two(x, carry):
        center = out_next[x]
        out_after[x] = 2.0 * center - ext_a[x + 4, 8 : 8 + ny, :] + speed[x] * laplace_z(center)
        return carry

    lax.fori_loop(0, nx, inner_two, 0, unroll=WAVE_UNROLL)
    for c in copies_b:
        c.arrive()
    unpack_wave(ext_b, recv_b)

    def step_two(x, carry):
        center = out_next[x]
        value = out_after[x] + speed[x] * laplace_xy(ext_b, x, ny)
        out_after[x] = value
        gradient = prior[x] + src[0, x] * center + src[1, x] * value
        out_grad[x] = gradient
        grad[x + 4, 0:ny, :] = gradient.astype(BF16)
        return carry

    lax.fori_loop(0, nx, step_two, 0, unroll=WAVE_UNROLL)
    for c in copies_g[:2]:
        c.start()
    for t in range(groups):
        for side, at in ((0, 0), (1, ny - 4)):
            pack_g[side, t] = jnp.concatenate(
                [out_grad[4 * t + j, at : at + 4, :] for j in range(4)], axis=0
            ).astype(BF16)
    for c in copies_g[2:]:
        c.start()
    for c in copies_g:
        c.arrive()
    for t in range(groups + 2):
        low = recv_g[0, t].astype(F32)
        high = recv_g[1, t].astype(F32)
        for j in range(4):
            grad[4 * t + j, ny : 2 * ny, :] = jnp.concatenate(
                [low[4 * j : 4 * j + 4], high[4 * j : 4 * j + 4], jnp.zeros((ny - 8, depth), F32)],
                axis=0,
            ).astype(BF16)

    x_min = jnp.where(gx == 0, 0, -8)
    x_max = jnp.where(gx == n_gx - 1, nx, nx + 8)
    y_min = jnp.where(gy == 0, 0, -8)
    y_max = jnp.where(gy == n_gy - 1, ny, ny + 8)

    def conv_plane(weight, rhs, rows):
        res = jnp.dot(weight[...], rhs, preferred_element_type=F32)
        return (
            res[rows : 2 * rows] + shift_z(res[:rows], -1) + shift_z(res[2 * rows :], 1)
        )

    def hidden(value, bias, rows, first, x):
        y = (lax.broadcasted_iota(jnp.int32, value.shape, 0) >> 3) + first
        inside = (y >= y_min) & (y < y_max) & (x >= x_min) & (x < x_max)
        full = jnp.concatenate([jnp.broadcast_to(bias, (8, depth))] * rows, axis=0)
        return jnp.where(inside, jnp.maximum(value + full, 0.0), 0.0).astype(BF16)

    def layer_one(p, carry):
        rhs = grad[pl.ds(p + 1, 3)].reshape(6 * ny, depth)
        h1[p] = hidden(conv_plane(w1, rhs, m1), b1, r1, -2, p - 2)
        return carry

    lax.fori_loop(0, nx + 4, layer_one, 0, unroll=UNROLL)

    def layer_two(p, carry):
        rhs = h1[pl.ds(p, 3)].reshape(3 * m1, depth)
        h2[p] = hidden(conv_plane(w2, rhs, m2), b2, r2, -1, p - 1)
        return carry

    lax.fori_loop(0, nx + 2, layer_two, 0, unroll=UNROLL)

    zero = jnp.zeros((ny, depth), F32)

    def layer_three(p, carry):
        gg, gd, dd = carry
        rhs = h2[pl.ds(p, 3)].reshape(3 * m2, depth)
        g = out_grad[p]
        d = conv_plane(w3, rhs, ny) + g
        out_step[p] = d
        return gg + g * g, gd + g * d, dd + d * d

    sums = lax.fori_loop(0, nx, layer_three, (zero, zero, zero), unroll=UNROLL)
    row = lax.broadcasted_iota(jnp.int32, (8, depth), 0)
    tile = jnp.zeros((8, depth), F32)
    for i, s in enumerate(sums):
        tile = jnp.where(row == i, jnp.sum(s, axis=0, keepdims=True), tile)
    folded = tile[:, 0:128]
    for i in range(1, depth // 128):
        folded = folded + tile[:, 128 * i : 128 * i + 128]

    def reduce_over(value, slot, slots, me, n, sends, recvs, peer_id):
        part[slot] = value
        slots[me] = value
        todo = []
        for i in range(1, n):
            c = pltpu.make_async_remote_copy(
                src_ref=part.at[slot],
                dst_ref=slots.at[me],
                send_sem=sends.at[i],
                recv_sem=recvs.at[i],
                device_id=peer_id(lax.rem(me + i, n)),
                device_id_type=MESH,
            )
            c.start()
            todo.append(c)
        for i, c in enumerate(todo):
            back = pltpu.make_async_remote_copy(
                src_ref=part.at[slot],
                dst_ref=slots.at[lax.rem(me + n - (i + 1), n)],
                send_sem=sends.at[i + 1],
                recv_sem=recvs.at[i + 1],
                device_id=peer_id(lax.rem(me + i + 1, n)),
                device_id_type=MESH,
            )
            back.wait_recv()
        total = slots[0]
        for i in range(1, n):
            total = total + slots[i]
        return total, todo

    over_y, todo_y = reduce_over(folded, 0, red_y, gy, n_gy, ry_send, ry_recv, lambda j: (gx, j))
    total, todo_x = reduce_over(over_y, 1, red_x, gx, n_gx, rx_send, rx_recv, lambda j: (j, gy))
    sums = jnp.sum(total, axis=1, keepdims=True)
    damping = 8.0 * float(nx * n_gx * ny * n_gy * depth)
    scale = sums[1:2] / (sums[0:1] + sums[2:3] + damping)

    def finish(p, carry):
        out_step[p] = scale * out_step[p]
        return carry

    lax.fori_loop(0, nx, finish, 0, unroll=4)
    for group in (copies_a, copies_b, copies_g):
        for c in group:
            c.sent()
    for c in todo_y + todo_x:
        c.wait_send()


def hand_on(*refs):
    for source, target in zip(refs[:4], refs[4:]):
        target[...] = source[...]


def shards(n_gx, n_gy, speed, before, now, src, prior, w_first, b_first, w_mid, b_mid, w_last):
    nx, ny, depth = now.shape
    out = jax.ShapeDtypeStruct(now.shape, F32)
    vmem = pl.BlockSpec(memory_space=pltpu.VMEM)
    half, groups = nx // 2, nx // 4
    r1, r2 = ny + 4, ny + 2
    ch = b_first.shape[0]
    outs = pl.pallas_call(
        functools.partial(kernel, n_gx, n_gy),
        out_shape=(out,) * 4,
        in_specs=[pl.BlockSpec(memory_space=pl.ANY)] * 5 + [vmem] * 3,
        out_specs=(vmem,) * 4,
        scratch_shapes=[
            pltpu.VMEM(now.shape, F32),
            pltpu.VMEM(now.shape, F32),
            pltpu.VMEM(src.shape, F32),
            pltpu.VMEM(now.shape, F32),
            pltpu.SemaphoreType.DMA((5,)),
            pltpu.VMEM((nx + 8, ny + 16, depth), F32),
            pltpu.VMEM((nx + 8, ny + 16, depth), F32),
            pltpu.VMEM((2, half, 8, depth), F32),
            pltpu.VMEM((2, half, 8, depth), F32),
            pltpu.VMEM((2, half, 8, depth), F32),
            pltpu.VMEM((2, half, 8, depth), F32),
            pltpu.VMEM((nx + 8, 2 * ny, depth), BF16),
            pltpu.VMEM((2, groups, 16, depth), BF16),
            pltpu.VMEM((2, groups + 2, 16, depth), BF16),
            pltpu.VMEM((nx + 4, r1 * ch, depth), BF16),
            pltpu.VMEM((nx + 2, r2 * ch, depth), BF16),
            pltpu.VMEM((3 * r1 * ch, 6 * ny), BF16),
            pltpu.VMEM((3 * r2 * ch, 3 * r1 * ch), BF16),
            pltpu.VMEM((3 * ny, 3 * r2 * ch), BF16),
            pltpu.VMEM((2, 8, 128), F32),
            pltpu.VMEM((n_gy, 8, 128), F32),
            pltpu.VMEM((n_gx, 8, 128), F32),
            pltpu.SemaphoreType.DMA((16,)),
            pltpu.SemaphoreType.DMA((16,)),
            pltpu.SemaphoreType.DMA((n_gy,)),
            pltpu.SemaphoreType.DMA((n_gy,)),
            pltpu.SemaphoreType.DMA((n_gx,)),
            pltpu.SemaphoreType.DMA((n_gx,)),
        ],
        compiler_params=pltpu.CompilerParams(
            collective_id=0, has_side_effects=True, vmem_limit_bytes=60 * 1024 * 1024
        ),
    )(
        speed,
        before,
        now,
        src,
        prior,
        jnp.concatenate([w_mid, w_last, w_first.reshape(27, ch, 1)], axis=2),
        b_first.reshape(1, ch),
        b_mid.reshape(1, ch),
    )
    block = pl.BlockSpec((nx // 4, ny, depth), lambda i: (i, 0, 0))
    return pl.pallas_call(
        hand_on,
        grid=(4,),
        out_shape=(out,) * 4,
        in_specs=[block] * 4,
        out_specs=(block,) * 4,
    )(*outs)


def solution(mesh):
    brick = P("gx", "gy", None)
    return jax.shard_map(
        functools.partial(shards, mesh.shape["gx"], mesh.shape["gy"]),
        mesh=mesh,
        in_specs=(brick, brick, brick, P(None, "gx", "gy", None), brick, P(), P(), P(), P(), P()),
        out_specs=(brick,) * 4,
        check_vma=False,
    )
```
